32 devices in a mesh: wide: 8 (over z, x), narrow: 4 (over y, core).
Axes of the slice: x: 2, y: 2, z: 4, core: 2. Of those that a mesh axis runs over, the one named last changes fastest.
Arguments:
- record: float32 [128, 128, 64, 128], P('wide', 'narrow'), may hold values from -6 to 6
Outputs:
- spectrum: float32 [2, 128, 4, 32, 64, 128], P(None, 'wide', 'narrow')
The draws below stay inside these ranges and needn't reach their ends.
All inputs are finite; a program needn't handle non-finite values.
Results may differ from the reference program's by a relative error of at most 0.00007.
Values sent between devices are 32-bit elements; how exact they have to be, the bound alone decides.
A program may use at most 192 MiB of HBM per device.

```python
import jax
import jax.numpy as jnp
import numpy as np

F_A = 128
F_B = 128
F_C = 64
F_D = 128
N_NARROW = 4


def block_levels(stream_key, dims, split, low, largest):
    def one(axis_at, parts):
        heights = jax.random.uniform(jax.random.fold_in(jax.random.fold_in(stream_key, 6), axis_at), (parts,), jnp.float32, low / len(split), largest / len(split))
        return jnp.repeat(jnp.exp(heights), dims[axis_at] // parts).reshape((-1,) + (1,) * (len(dims) - axis_at - 1))

    level = one(*split[0])
    for cut in split[1:]:
        level = level * one(*cut)
    return level


def scatter_about(own_key, extent, spread, limit, pieces=(), kind=jnp.bfloat16):
    array = jax.random.normal(own_key, extent, jnp.float32) * spread
    if len(pieces) > 0:
        array = block_levels(own_key, extent, pieces, -0.22, 0.18) * array
    return jnp.clip(array, min=-limit, max=limit).astype(kind)


def setup_inputs(seed: int = 0) -> dict:
    arg_keys = jax.random.split(jax.random.key(seed), 2)
    return {
        "record": scatter_about(arg_keys[0], (F_A, F_B, F_C, F_D), 1.0, 6.0, ((0, 8), (1, 4)), jnp.float32),
    }


def reversed_digits(number, bit_count):
    result = 0 * number
    for position in range(bit_count):
        result = result + ((number // (1 << position)) % 2) * (1 << (bit_count - 1 - position))
    return result


def reference(record):
    spectrum = jnp.fft.fft(record.reshape(-1), norm="ortho")
    levels = N_NARROW.bit_length() - 1
    local_b = F_B // N_NARROW
    residue_order = jnp.asarray(reversed_digits(np.arange(N_NARROW), levels), dtype=jnp.int32)
    halves = []
    for component in (jnp.real(spectrum), jnp.imag(spectrum)):
        arranged = component.reshape(F_D, F_C, local_b, N_NARROW, F_A)
        arranged = jnp.take(arranged, residue_order, axis=3)
        halves.append(jnp.transpose(arranged, (4, 3, 2, 1, 0)))
    return jnp.stack(halves)
```

```python
import functools
import math

import jax
import jax.numpy as jnp
from jax import lax
from jax.experimental import pallas as pl
from jax.experimental.pallas import tpu as pltpu
from jax.sharding import PartitionSpec as P

SPLIT = lax.Precision.HIGH
TWO_PI = 2.0 * math.pi
CHUNKS = 8


def swap(block, axis, place):
    count = lax.axis_size(axis)
    return lax.ppermute(block, axis, [(at, at ^ (1 << place)) for at in range(count)])


def turn(phases, length):
    angles = (phases % length).astype(jnp.float32) * (TWO_PI / length)
    return jnp.cos(angles), jnp.sin(angles)


def reversed_digits(number, bit_count):
    result = 0 * number
    for position in range(bit_count):
        result = result + number // (1 << position) % 2 * (1 << bit_count - 1 - position)
    return result


def halves(values, upper):
    size = values.shape[-2] // 2
    axis = values.ndim - 2
    keep = lax.dynamic_slice_in_dim(values, upper * size, size, axis)
    send = lax.dynamic_slice_in_dim(values, (1 - upper) * size, size, axis)
    return keep, send


def two_parts(table):
    high = lax.reduce_precision(table, 8, 7)
    low = lax.reduce_precision(table - high, 8, 7)
    return high.astype(jnp.bfloat16), low.astype(jnp.bfloat16)


def last_factors(pieces, group, *refs):
    blocks = refs[:pieces]
    turn_p, turn_m, table_c, turn_c, table_d, out = refs[pieces:]
    count_m = out.shape[2]
    size_d = out.shape[4]
    size_c = out.shape[3]
    cos_p, sin_p = turn_p[0, 0], turn_p[1, 0]
    cos_c, sin_c = turn_c[0], turn_c[1]

    def parts(values):
        high = values.astype(jnp.bfloat16)
        low = (values - high.astype(jnp.float32)).astype(jnp.bfloat16)
        return high, low

    def body(step, carry):
        columns = []
        for index in range(group):
            m = step * group + index
            real = jnp.concatenate([block[0, 0, m] for block in blocks], axis=0)
            imag = jnp.concatenate([block[0, 1, m] for block in blocks], axis=0)
            cos_m, sin_m = turn_m[0, m], turn_m[1, m]
            cosine = cos_p * cos_m - sin_p * sin_m
            sines = sin_p * cos_m + cos_p * sin_m
            columns.append(
                jnp.concatenate(
                    [real * cosine + imag * sines, imag * cosine - real * sines], axis=0
                )
            )
        wide = jnp.concatenate(columns, axis=1)
        high, low = parts(wide)
        third = jnp.dot(
            table_c[...],
            jnp.concatenate([high, low, high], axis=0),
            preferred_element_type=jnp.float32,
        )
        rows = []
        for index in range(group):
            part = third[:, index * size_d : (index + 1) * size_d]
            real, imag = part[:size_c], part[size_c:]
            rows.append(
                jnp.concatenate(
                    [real * cos_c + imag * sin_c, imag * cos_c - real * sin_c], axis=1
                )
            )
        tall = jnp.concatenate(rows, axis=0)
        high, low = parts(tall)
        fourth = jnp.dot(
            jnp.concatenate([high, low, high], axis=1),
            table_d[...],
            preferred_element_type=jnp.float32,
        )
        for index in range(group):
            part = fourth[index * size_c : (index + 1) * size_c]
            m = step * group + index
            out[0, 0, m] = part[:, :size_d]
            out[1, 0, m] = part[:, size_d:]
        return carry

    lax.fori_loop(0, count_m // group, body, 0)


def finish(sections, turn_p, turn_m, table_c, turn_c, table_d):
    count_p, _, count_m, share_c, size_d = sections[0].shape
    pieces = len(sections)
    size_c = share_c * pieces
    group = math.gcd(count_m, 4)
    piece = pl.BlockSpec((1, 2, count_m, share_c, size_d), lambda p: (p, 0, 0, 0, 0))
    whole = lambda table: pl.BlockSpec(table.shape, lambda p: (0,) * table.ndim)
    return pl.pallas_call(
        functools.partial(last_factors, pieces, group),
        grid=(count_p,),
        out_shape=jax.ShapeDtypeStruct((2, count_p, count_m, size_c, size_d), jnp.float32),
        in_specs=[piece] * pieces
        + [
            pl.BlockSpec((2, 1, size_c, size_d), lambda p: (0, p, 0, 0)),
            whole(turn_m),
            whole(table_c),
            whole(turn_c),
            whole(table_d),
        ],
        out_specs=pl.BlockSpec((2, 1, count_m, size_c, size_d), lambda p: (0, p, 0, 0, 0)),
        compiler_params=pltpu.CompilerParams(vmem_limit_bytes=40 * 1024 * 1024),
        cost_estimate=pl.CostEstimate(
            flops=2 * 3 * count_p * count_m * size_c * size_d * 2 * 2 * (size_c + size_d),
            bytes_accessed=16 * count_p * count_m * size_c * size_d,
            transcendentals=0,
        ),
        name="last_factors",
    )(*sections, turn_p, turn_m, table_c, turn_c, table_d)


def shards(record):
    local_a, local_b, size_c, size_d = record.shape
    wide_size = lax.axis_size("wide")
    narrow_size = lax.axis_size("narrow")
    narrow_levels = narrow_size.bit_length() - 1
    levels = wide_size.bit_length() - 2
    size_a = local_a * wide_size
    size_b = local_b * narrow_size
    total_count = size_a * size_b * size_c * size_d
    inner = size_c * size_d
    wide_at = lax.axis_index("wide")
    narrow_at = lax.axis_index("narrow")
    bits = [wide_at // (1 << place) % 2 for place in range(levels)]
    share_c = size_c // CHUNKS

    def positions(slots):
        return (
            local_a * (wide_at ^ jnp.arange(slots, dtype=jnp.int32))[:, None]
            + jnp.arange(local_a, dtype=jnp.int32)
        )

    inputs_a = positions(wide_size).reshape(-1)
    outputs_a = positions(wide_size // 2)[:, :, None]
    cosine, sines = turn(
        outputs_a * (inputs_a * narrow_size + narrow_at), size_a * narrow_size
    )
    scale = 1.0 / math.sqrt(total_count)
    table_a = (jnp.stack([cosine, -sines], axis=1) * scale).reshape(-1, size_a)

    own_p = local_a * wide_at + jnp.arange(local_a, dtype=jnp.int32)
    index_m = jnp.arange(local_b, dtype=jnp.int32)
    outputs_b = narrow_size * index_m + reversed_digits(narrow_at, narrow_levels)
    mask = 0
    left_b = local_b
    for bit in bits:
        left_b //= 2
        mask = mask + bit * left_b
    inputs_b = jnp.arange(local_b, dtype=jnp.int32) ^ mask
    frequency = own_p[:, None] + size_a * outputs_b[None, :]
    cosine, sines = turn(frequency[:, :, None] * inputs_b, size_a * size_b)
    table_b = jnp.stack(
        [jnp.stack([cosine, sines], axis=2), jnp.stack([-sines, cosine], axis=2)], axis=1
    )

    offset = jnp.arange(inner, dtype=jnp.int32).reshape(size_c, size_d)
    turn_p = jnp.stack(turn(own_p[:, None, None] * offset, total_count))
    turn_m = jnp.stack(turn(outputs_b[:, None, None] * offset, size_b * inner))
    index_c = jnp.arange(size_c, dtype=jnp.int32)
    index_d = jnp.arange(size_d, dtype=jnp.int32)
    cosine, sines = turn(index_c[:, None] * index_c, size_c)
    high, low = two_parts(jnp.block([[cosine, sines], [-sines, cosine]]))
    table_c = jnp.concatenate([high, high, low], axis=1)
    turn_c = jnp.stack(turn(index_c[:, None] * index_d, inner))
    cosine, sines = turn(index_d[:, None] * index_d, size_d)
    high, low = two_parts(jnp.block([[cosine, -sines], [sines, cosine]]))
    table_d = jnp.concatenate([high, high, low], axis=0)

    sections = []
    for chunk in range(CHUNKS):
        values = lax.slice_in_dim(record, chunk * share_c, (chunk + 1) * share_c, axis=2)
        values = values.reshape(local_a, local_b * share_c, size_d)
        for place in range(levels):
            keep, send = halves(values, bits[place])
            values = jnp.concatenate([keep, swap(send, "wide", place)], axis=0)
        values = jnp.concatenate([values, swap(values, "wide", levels)], axis=0)
        rows = values.shape[1]
        spread = jnp.einsum(
            "pa,an->pn", table_a, values.reshape(size_a, rows * size_d), precision=SPLIT
        ).reshape(wide_size // 2, 2, local_a, rows, size_d)
        for place in reversed(range(levels)):
            half = spread.shape[0] // 2
            mine, other = spread[:half], swap(spread[half:], "wide", place)
            spread = jnp.concatenate([mine, other], axis=3)
            if mine.shape[3] < share_c:
                spread = jnp.where(
                    bits[place] > 0, jnp.concatenate([other, mine], axis=3), spread
                )
        current = spread[0]
        for place in reversed(range(narrow_levels)):
            partner = swap(current, "narrow", place)
            upper = narrow_at // (1 << place) % 2
            current = partner + (1 - 2 * upper).astype(jnp.float32) * current
            if place > 0:
                cosine, sines = turn(upper * (narrow_at % (1 << place)), 2 << place)
                current = jnp.stack(
                    [
                        current[0] * cosine + current[1] * sines,
                        current[1] * cosine - current[0] * sines,
                    ]
                )
        current = current.reshape(2, local_a, local_b, share_c * size_d)
        section = jnp.einsum("aomib,iabn->aomn", table_b, current, precision=SPLIT)
        sections.append(section.reshape(local_a, 2, local_b, share_c, size_d))
    result = finish(sections, turn_p, turn_m, table_c, turn_c, table_d)
    return result.reshape(2, local_a, 1, local_b, size_c, size_d)


def solution(mesh):
    return jax.shard_map(
        shards,
        mesh=mesh,
        in_specs=(P("wide", "narrow", None, None),),
        out_specs=P(None, "wide", "narrow", None, None, None),
        check_vma=False,
    )
```

```python
import functools
import math

import jax
import jax.numpy as jnp
from jax import lax
from jax.experimental import pallas as pl
from jax.experimental.pallas import tpu as pltpu
from jax.sharding import PartitionSpec as P

SPLIT = lax.Precision.HIGH
TWO_PI = 2.0 * math.pi
CHUNKS = 8
SPLIT_B = 2


def swap(block, axis, place):
    count = lax.axis_size(axis)
    return lax.ppermute(block, axis, [(at, at ^ (1 << place)) for at in range(count)])


def turn(phases, length):
    angles = (phases % length).astype(jnp.float32) * (TWO_PI / length)
    return jnp.cos(angles), jnp.sin(angles)


def reversed_digits(number, bit_count):
    result = 0 * number
    for position in range(bit_count):
        result = result + number // (1 << position) % 2 * (1 << bit_count - 1 - position)
    return result


def halves(values, upper):
    size = values.shape[-2] // 2
    axis = values.ndim - 2
    keep = lax.dynamic_slice_in_dim(values, upper * size, size, axis)
    send = lax.dynamic_slice_in_dim(values, (1 - upper) * size, size, axis)
    return keep, send


def two_parts(table):
    high = lax.reduce_precision(table, 8, 7)
    low = lax.reduce_precision(table - high, 8, 7)
    return high.astype(jnp.bfloat16), low.astype(jnp.bfloat16)


def last_factors(pieces, group, *refs):
    blocks = refs[:pieces]
    turn_p, turn_m, table_c, turn_c, table_d, out = refs[pieces:]
    count_m = out.shape[2]
    size_d = out.shape[4]
    size_c = out.shape[3]
    cos_p, sin_p = turn_p[0, 0], turn_p[1, 0]
    cos_c, sin_c = turn_c[0], turn_c[1]

    def parts(values):
        high = values.astype(jnp.bfloat16)
        low = (values - high.astype(jnp.float32)).astype(jnp.bfloat16)
        return high, low

    def body(step, carry):
        columns = []
        for index in range(group):
            m = step * group + index
            real = jnp.concatenate([block[0, 0, m] for block in blocks], axis=0)
            imag = jnp.concatenate([block[0, 1, m] for block in blocks], axis=0)
            cos_m, sin_m = turn_m[0, m], turn_m[1, m]
            cosine = cos_p * cos_m - sin_p * sin_m
            sines = sin_p * cos_m + cos_p * sin_m
            columns.append(
                jnp.concatenate(
                    [real * cosine + imag * sines, imag * cosine - real * sines], axis=0
                )
            )
        wide = jnp.concatenate(columns, axis=1)
        high, low = parts(wide)
        third = jnp.dot(
            table_c[...],
            jnp.concatenate([high, low, high], axis=0),
            preferred_element_type=jnp.float32,
        )
        rows = []
        for index in range(group):
            part = third[:, index * size_d : (index + 1) * size_d]
            real, imag = part[:size_c], part[size_c:]
            rows.append(
                jnp.concatenate(
                    [real * cos_c + imag * sin_c, imag * cos_c - real * sin_c], axis=1
                )
            )
        tall = jnp.concatenate(rows, axis=0)
        high, low = parts(tall)
        fourth = jnp.dot(
            jnp.concatenate([high, low, high], axis=1),
            table_d[...],
            preferred_element_type=jnp.float32,
        )
        for index in range(group):
            part = fourth[index * size_c : (index + 1) * size_c]
            m = step * group + index
            out[0, 0, m] = part[:, :size_d]
            out[1, 0, m] = part[:, size_d:]
        return carry

    lax.fori_loop(0, count_m // group, body, 0)


def finish(sections, turn_p, turn_m, table_c, turn_c, table_d):
    count_p, _, count_m, share_c, size_d = sections[0].shape
    pieces = len(sections)
    size_c = share_c * pieces
    group = math.gcd(count_m, 4)
    piece = pl.BlockSpec((1, 2, count_m, share_c, size_d), lambda p: (p, 0, 0, 0, 0))
    whole = lambda table: pl.BlockSpec(table.shape, lambda p: (0,) * table.ndim)
    return pl.pallas_call(
        functools.partial(last_factors, pieces, group),
        grid=(count_p,),
        out_shape=jax.ShapeDtypeStruct((2, count_p, count_m, size_c, size_d), jnp.float32),
        in_specs=[piece] * pieces
        + [
            pl.BlockSpec((2, 1, size_c, size_d), lambda p: (0, p, 0, 0)),
            whole(turn_m),
            whole(table_c),
            whole(turn_c),
            whole(table_d),
        ],
        out_specs=pl.BlockSpec((2, 1, count_m, size_c, size_d), lambda p: (0, p, 0, 0, 0)),
        compiler_params=pltpu.CompilerParams(vmem_limit_bytes=40 * 1024 * 1024),
        cost_estimate=pl.CostEstimate(
            flops=2 * 3 * count_p * count_m * size_c * size_d * 2 * 2 * (size_c + size_d),
            bytes_accessed=16 * count_p * count_m * size_c * size_d,
            transcendentals=0,
        ),
        name="last_factors",
    )(*sections, turn_p, turn_m, table_c, turn_c, table_d)


def shards(record):
    local_a, local_b, size_c, size_d = record.shape
    wide_size = lax.axis_size("wide")
    narrow_size = lax.axis_size("narrow")
    narrow_levels = narrow_size.bit_length() - 1
    levels = wide_size.bit_length() - 2
    size_a = local_a * wide_size
    size_b = local_b * narrow_size
    total_count = size_a * size_b * size_c * size_d
    inner = size_c * size_d
    wide_at = lax.axis_index("wide")
    narrow_at = lax.axis_index("narrow")
    bits = [wide_at // (1 << place) % 2 for place in range(levels)]
    share_c = size_c // CHUNKS
    share_b = local_b // SPLIT_B

    def positions(slots):
        return (
            local_a * (wide_at ^ jnp.arange(slots, dtype=jnp.int32))[:, None]
            + jnp.arange(local_a, dtype=jnp.int32)
        )

    inputs_a = positions(wide_size).reshape(-1)
    outputs_a = positions(wide_size // 2)[:, :, None]
    cosine, sines = turn(
        outputs_a * (inputs_a * narrow_size + narrow_at), size_a * narrow_size
    )
    scale = 1.0 / math.sqrt(total_count)
    table_a = (jnp.stack([cosine, -sines], axis=1) * scale).reshape(-1, size_a)

    own_p = local_a * wide_at + jnp.arange(local_a, dtype=jnp.int32)
    index_m = jnp.arange(local_b, dtype=jnp.int32)
    outputs_b = narrow_size * index_m + reversed_digits(narrow_at, narrow_levels)
    mask = 0
    left_b = share_b
    for bit in bits:
        left_b //= 2
        mask = mask + bit * left_b
    inputs_b = jnp.arange(local_b, dtype=jnp.int32) ^ mask
    frequency = own_p[:, None] + size_a * outputs_b[None, :]
    cosine, sines = turn(frequency[:, :, None] * inputs_b, size_a * size_b)
    table_b = jnp.stack(
        [jnp.stack([cosine, sines], axis=2), jnp.stack([-sines, cosine], axis=2)], axis=1
    )

    offset = jnp.arange(inner, dtype=jnp.int32).reshape(size_c, size_d)
    turn_p = jnp.stack(turn(own_p[:, None, None] * offset, total_count))
    turn_m = jnp.stack(turn(outputs_b[:, None, None] * offset, size_b * inner))
    index_c = jnp.arange(size_c, dtype=jnp.int32)
    index_d = jnp.arange(size_d, dtype=jnp.int32)
    cosine, sines = turn(index_c[:, None] * index_c, size_c)
    high, low = two_parts(jnp.block([[cosine, sines], [-sines, cosine]]))
    table_c = jnp.concatenate([high, high, low], axis=1)
    turn_c = jnp.stack(turn(index_c[:, None] * index_d, inner))
    cosine, sines = turn(index_d[:, None] * index_d, size_d)
    high, low = two_parts(jnp.block([[cosine, -sines], [sines, cosine]]))
    table_d = jnp.concatenate([high, high, low], axis=0)

    def slab(chunk):
        low_b, low_c = chunk % SPLIT_B * share_b, chunk // SPLIT_B * share_c
        values = record[:, low_b : low_b + share_b, low_c : low_c + share_c, :]
        return values.reshape(local_a, share_b * share_c, size_d)

    def stage(step, keep, other):
        if step <= levels:
            values = keep if step == 0 else jnp.concatenate([keep, other], axis=0)
            if step == levels:
                return values, values, ("wide", levels)
            return *halves(values, bits[step]), ("wide", step)
        step -= levels + 1
        if step <= levels:
            if step == 0:
                values = jnp.concatenate([keep, other], axis=0)
                spread = jnp.einsum("pa,ard->prd", table_a, values, precision=SPLIT).reshape(
                    wide_size // 2, 2, local_a, values.shape[1], size_d
                )
            else:
                spread = jnp.concatenate([keep, other], axis=3)
                if keep.shape[3] < share_c:
                    spread = jnp.where(
                        bits[levels - step] > 0,
                        jnp.concatenate([other, keep], axis=3),
                        spread,
                    )
            if step < levels:
                half = spread.shape[0] // 2
                return spread[:half], spread[half:], ("wide", levels - 1 - step)
            return spread[0], spread[0], ("narrow", narrow_levels - 1)
        place = narrow_levels + levels - step
        upper = narrow_at // (1 << place) % 2
        current = other + (1 - 2 * upper).astype(jnp.float32) * keep
        if place == 0:
            return current, None, None
        cosine, sines = turn(upper * (narrow_at % (1 << place)), 2 << place)
        current = jnp.stack(
            [
                current[0] * cosine + current[1] * sines,
                current[1] * cosine - current[0] * sines,
            ]
        )
        return current, current, ("narrow", place - 1)

    count = CHUNKS * SPLIT_B
    steps = 2 * levels + 2 + narrow_levels
    starts = [0.35 * step - 0.5 for step in range(levels + 1)]
    starts += [1.4 + 0.35 * levels + 0.7 * step for step in range(levels + 1)]
    starts += [starts[-1] + 0.14 + 1.4 * step for step in range(1, narrow_levels)]
    starts += [starts[-1] + 0.14]
    if narrow_levels > 1:
        starts[-1] = starts[-2] + 0.14
    plan = sorted(
        ((chunk + starts[step], chunk, step) for chunk in range(count) for step in range(steps))
    )
    held = {}
    before = None
    for _, chunk, step in plan:
        keep, other = held.pop(chunk) if step else (slab(chunk), None)
        if before is not None and before != chunk:
            rest = held[before][0]
            if other is None:
                keep, rest = lax.optimization_barrier((keep, rest))
            else:
                keep, other, rest = lax.optimization_barrier((keep, other, rest))
            held[before] = (rest, held[before][1])
        keep, send, way = stage(step, keep, other)
        held[chunk] = (keep, None if send is None else swap(send, *way))
        before = chunk

    sections = []
    for chunk in range(CHUNKS):
        current = jnp.concatenate(
            [
                held[chunk * SPLIT_B + part][0].reshape(2, local_a, share_b, share_c, size_d)
                for part in range(SPLIT_B)
            ],
            axis=2,
        )
        section = jnp.einsum("aomib,iabcd->aomcd", table_b, current, precision=SPLIT)
        sections.append(section)
    result = finish(sections, turn_p, turn_m, table_c, turn_c, table_d)
    return result.reshape(2, local_a, 1, local_b, size_c, size_d)


def solution(mesh):
    return jax.shard_map(
        shards,
        mesh=mesh,
        in_specs=(P("wide", "narrow", None, None),),
        out_specs=P(None, "wide", "narrow", None, None, None),
        check_vma=False,
    )
```

```python
import functools
import math

import jax
import jax.numpy as jnp
from jax import lax
from jax.experimental import pallas as pl
from jax.experimental.pallas import tpu as pltpu
from jax.sharding import PartitionSpec as P

SPLIT = lax.Precision.HIGH
TWO_PI = 2.0 * math.pi
CHUNKS = 8
SPLIT_B = 2


def swap(block, axis, place):
    count = lax.axis_size(axis)
    return lax.ppermute(block, axis, [(at, at ^ (1 << place)) for at in range(count)])


def turn(phases, length):
    angles = (phases % length).astype(jnp.float32) * (TWO_PI / length)
    return jnp.cos(angles), jnp.sin(angles)


def reversed_digits(number, bit_count):
    result = 0 * number
    for position in range(bit_count):
        result = result + number // (1 << position) % 2 * (1 << bit_count - 1 - position)
    return result


def halves(values, upper):
    size = values.shape[-2] // 2
    axis = values.ndim - 2
    keep = lax.dynamic_slice_in_dim(values, upper * size, size, axis)
    send = lax.dynamic_slice_in_dim(values, (1 - upper) * size, size, axis)
    return keep, send


def two_parts(table):
    high = lax.reduce_precision(table, 8, 7)
    low = lax.reduce_precision(table - high, 8, 7)
    return high.astype(jnp.bfloat16), low.astype(jnp.bfloat16)


def last_factors(pieces, group, *refs):
    blocks = refs[:pieces]
    turn_p, turn_m, table_c, turn_c, table_d, out = refs[pieces:]
    count_m = out.shape[2]
    size_d = out.shape[4]
    size_c = out.shape[3]
    cos_p, sin_p = turn_p[0, 0], turn_p[1, 0]
    cos_c, sin_c = turn_c[0], turn_c[1]

    def parts(values):
        high = values.astype(jnp.bfloat16)
        low = (values - high.astype(jnp.float32)).astype(jnp.bfloat16)
        return high, low

    def body(step, carry):
        columns = []
        for index in range(group):
            m = step * group + index
            real = jnp.concatenate([block[0, 0, m] for block in blocks], axis=0)
            imag = jnp.concatenate([block[0, 1, m] for block in blocks], axis=0)
            cos_m, sin_m = turn_m[0, m], turn_m[1, m]
            cosine = cos_p * cos_m - sin_p * sin_m
            sines = sin_p * cos_m + cos_p * sin_m
            columns.append(
                jnp.concatenate(
                    [real * cosine + imag * sines, imag * cosine - real * sines], axis=0
                )
            )
        wide = jnp.concatenate(columns, axis=1)
        high, low = parts(wide)
        third = jnp.dot(
            table_c[...],
            jnp.concatenate([high, low, high], axis=0),
            preferred_element_type=jnp.float32,
        )
        rows = []
        for index in range(group):
            part = third[:, index * size_d : (index + 1) * size_d]
            real, imag = part[:size_c], part[size_c:]
            rows.append(
                jnp.concatenate(
                    [real * cos_c + imag * sin_c, imag * cos_c - real * sin_c], axis=1
                )
            )
        tall = jnp.concatenate(rows, axis=0)
        high, low = parts(tall)
        fourth = jnp.dot(
            jnp.concatenate([high, low, high], axis=1),
            table_d[...],
            preferred_element_type=jnp.float32,
        )
        for index in range(group):
            part = fourth[index * size_c : (index + 1) * size_c]
            m = step * group + index
            out[0, 0, m] = part[:, :size_d]
            out[1, 0, m] = part[:, size_d:]
        return carry

    lax.fori_loop(0, count_m // group, body, 0)


def finish(sections, turn_p, turn_m, table_c, turn_c, table_d):
    count_p, _, count_m, share_c, size_d = sections[0].shape
    pieces = len(sections)
    size_c = share_c * pieces
    group = math.gcd(count_m, 4)
    piece = pl.BlockSpec((1, 2, count_m, share_c, size_d), lambda p: (p, 0, 0, 0, 0))
    whole = lambda table: pl.BlockSpec(table.shape, lambda p: (0,) * table.ndim)
    return pl.pallas_call(
        functools.partial(last_factors, pieces, group),
        grid=(count_p,),
        out_shape=jax.ShapeDtypeStruct((2, count_p, count_m, size_c, size_d), jnp.float32),
        in_specs=[piece] * pieces
        + [
            pl.BlockSpec((2, 1, size_c, size_d), lambda p: (0, p, 0, 0)),
            whole(turn_m),
            whole(table_c),
            whole(turn_c),
            whole(table_d),
        ],
        out_specs=pl.BlockSpec((2, 1, count_m, size_c, size_d), lambda p: (0, p, 0, 0, 0)),
        compiler_params=pltpu.CompilerParams(vmem_limit_bytes=40 * 1024 * 1024),
        cost_estimate=pl.CostEstimate(
            flops=2 * 3 * count_p * count_m * size_c * size_d * 2 * 2 * (size_c + size_d),
            bytes_accessed=16 * count_p * count_m * size_c * size_d,
            transcendentals=0,
        ),
        name="last_factors",
    )(*sections, turn_p, turn_m, table_c, turn_c, table_d)


def shards(record):
    local_a, local_b, size_c, size_d = record.shape
    wide_size = lax.axis_size("wide")
    narrow_size = lax.axis_size("narrow")
    narrow_levels = narrow_size.bit_length() - 1
    levels = wide_size.bit_length() - 2
    size_a = local_a * wide_size
    size_b = local_b * narrow_size
    total_count = size_a * size_b * size_c * size_d
    inner = size_c * size_d
    wide_at = lax.axis_index("wide")
    narrow_at = lax.axis_index("narrow")
    bits = [wide_at // (1 << place) % 2 for place in range(levels)]
    share_c = size_c // CHUNKS
    share_b = local_b // SPLIT_B

    def positions(slots):
        return (
            local_a * (wide_at ^ jnp.arange(slots, dtype=jnp.int32))[:, None]
            + jnp.arange(local_a, dtype=jnp.int32)
        )

    inputs_a = positions(wide_size).reshape(-1)
    outputs_a = positions(wide_size // 2)[:, :, None]
    cosine, sines = turn(
        outputs_a * (inputs_a * narrow_size + narrow_at), size_a * narrow_size
    )
    scale = 1.0 / math.sqrt(total_count)
    table_a = (jnp.stack([cosine, -sines], axis=1) * scale).reshape(-1, size_a)

    own_p = local_a * wide_at + jnp.arange(local_a, dtype=jnp.int32)
    index_m = jnp.arange(local_b, dtype=jnp.int32)
    outputs_b = narrow_size * index_m + reversed_digits(narrow_at, narrow_levels)
    mask = 0
    left_b = share_b
    for bit in bits:
        left_b //= 2
        mask = mask + bit * left_b
    inputs_b = jnp.arange(local_b, dtype=jnp.int32) ^ mask
    frequency = own_p[:, None] + size_a * outputs_b[None, :]
    cosine, sines = turn(frequency[:, :, None] * inputs_b, size_a * size_b)
    table_b = jnp.stack(
        [jnp.stack([cosine, sines], axis=2), jnp.stack([-sines, cosine], axis=2)], axis=1
    )

    offset = jnp.arange(inner, dtype=jnp.int32).reshape(size_c, size_d)
    turn_p = jnp.stack(turn(own_p[:, None, None] * offset, total_count))
    turn_m = jnp.stack(turn(outputs_b[:, None, None] * offset, size_b * inner))
    index_c = jnp.arange(size_c, dtype=jnp.int32)
    index_d = jnp.arange(size_d, dtype=jnp.int32)
    cosine, sines = turn(index_c[:, None] * index_c, size_c)
    high, low = two_parts(jnp.block([[cosine, sines], [-sines, cosine]]))
    table_c = jnp.concatenate([high, high, low], axis=1)
    turn_c = jnp.stack(turn(index_c[:, None] * index_d, inner))
    cosine, sines = turn(index_d[:, None] * index_d, size_d)
    high, low = two_parts(jnp.block([[cosine, -sines], [sines, cosine]]))
    table_d = jnp.concatenate([high, high, low], axis=0)

    def slab(chunk):
        low_b, low_c = chunk % SPLIT_B * share_b, chunk // SPLIT_B * share_c
        values = record[:, low_b : low_b + share_b, low_c : low_c + share_c, :]
        return values.reshape(local_a, share_b * share_c, size_d)

    def stage(step, keep, other):
        if step <= levels:
            values = keep if step == 0 else jnp.concatenate([keep, other], axis=0)
            if step == levels:
                return values, values, ("wide", levels)
            return *halves(values, bits[step]), ("wide", step)
        step -= levels + 1
        if step <= levels:
            if step == 0:
                values = jnp.concatenate([keep, other], axis=0)
                spread = jnp.einsum("pa,ard->prd", table_a, values, precision=SPLIT).reshape(
                    wide_size // 2, 2, local_a, values.shape[1], size_d
                )
            else:
                spread = jnp.concatenate([keep, other], axis=3)
                if keep.shape[3] < share_c:
                    spread = jnp.where(
                        bits[levels - step] > 0,
                        jnp.concatenate([other, keep], axis=3),
                        spread,
                    )
            if step < levels:
                half = spread.shape[0] // 2
                return spread[:half], spread[half:], ("wide", levels - 1 - step)
            return spread[0], spread[0], ("narrow", narrow_levels - 1)
        place = narrow_levels + levels - step
        upper = narrow_at // (1 << place) % 2
        current = other + (1 - 2 * upper).astype(jnp.float32) * keep
        if place == 0:
            return current, None, None
        cosine, sines = turn(upper * (narrow_at % (1 << place)), 2 << place)
        current = jnp.stack(
            [
                current[0] * cosine + current[1] * sines,
                current[1] * cosine - current[0] * sines,
            ]
        )
        return current, current, ("narrow", place - 1)

    count = CHUNKS * SPLIT_B
    steps = 2 * levels + 2 + narrow_levels
    starts = [-1.3 - 0.96 * (levels - step) for step in range(levels + 1)]
    starts += [0.3 + 0.92 * step for step in range(levels + 1)]
    starts += [starts[-1] + 1.32 + 1.23 * step for step in range(narrow_levels)]
    starts = [round(start, 2) for start in starts]
    plan = sorted(
        ((chunk + starts[step], chunk, step) for chunk in range(count) for step in range(steps))
    )
    held = {}
    before = None
    for _, chunk, step in plan:
        keep, other = held.pop(chunk) if step else (slab(chunk), None)
        if before is not None and before != chunk:
            rest = held[before][0]
            if other is None:
                keep, rest = lax.optimization_barrier((keep, rest))
            else:
                keep, other, rest = lax.optimization_barrier((keep, other, rest))
            held[before] = (rest, held[before][1])
        keep, send, way = stage(step, keep, other)
        held[chunk] = (keep, None if send is None else swap(send, *way))
        before = chunk
        if step == steps - 1 and chunk % SPLIT_B == SPLIT_B - 1:
            first = chunk - SPLIT_B + 1
            current = jnp.concatenate(
                [
                    held[part][0].reshape(2, local_a, share_b, share_c, size_d)
                    for part in range(first, chunk + 1)
                ],
                axis=2,
            )
            section = jnp.einsum("aomib,iabcd->aomcd", table_b, current, precision=SPLIT)
            held[chunk] = (section, None)
    sections = [held[chunk * SPLIT_B + SPLIT_B - 1][0] for chunk in range(CHUNKS)]
    result = finish(sections, turn_p, turn_m, table_c, turn_c, table_d)
    return result.reshape(2, local_a, 1, local_b, size_c, size_d)


def solution(mesh):
    return jax.shard_map(
        shards,
        mesh=mesh,
        in_specs=(P("wide", "narrow", None, None),),
        out_specs=P(None, "wide", "narrow", None, None, None),
        check_vma=False,
    )
```
